32 devices in a mesh: groups: 2 (over y), node: 8 (over z, x), local: 2 (over core).
Axes of the slice: x: 2, y: 2, z: 4, core: 2. Of those that a mesh axis runs over, the one named last changes fastest.
Arguments:
- tokens: bfloat16 [2, 128, 7168], P(None, ('groups', 'node', 'local')), parts along dimension 1, may hold values from -6 to 6
- router: bfloat16 [7168, 16], replicated, may hold values from -0.25 to 0.25
- w_gate: bfloat16 [16, 7168, 2048], P('node', None, 'local'), may hold values from -0.0625 to 0.0625
- w_up: bfloat16 [16, 7168, 2048], P('node', None, 'local'), may hold values from -0.0625 to 0.0625
- w_down: bfloat16 [16, 2048, 7168], P('node', 'local'), may hold values from -0.25 to 0.25
- node_lists: int32 [2, 128, 4], P(None, ('groups', 'node', 'local')), parts along dimension 1, may hold values from 0 to 7, all different within a row; in each aligned block of 4 rows (0 to 3, 4 to 7, ..., all dimensions but the last counted through in order) at most 3 rows name the same one
Outputs:
- mixed: bfloat16 [2, 128, 7168], P(None, ('groups', 'node', 'local')), parts along dimension 1
The draws below stay inside these ranges and needn't reach their ends.
There are 2 independent parts, one for each index of `groups`. The reference program is written for one: setup_inputs(seed, part) draws one part's arguments, and reference() takes and returns one part's arrays. A program takes and returns all parts, laid end to end along the dimension named above; an argument that names none is the same for every part. Nothing has to cross between parts.
Inputs may be any that keep to these rules, and one draw needn't show every extreme that they name: `node_lists`: each token names 4 distinct node groups. Among the 4 tokens of one device in one micro-batch no node group is named more than 3 times, and in some devices' tokens some group is named exactly 3 times.
All inputs are finite; a program needn't handle non-finite values.
Results may differ from the reference program's by a relative error of at most 0.009.
Values may be sent and summed in bfloat16 or wider, within the bound.
A program may use at most 192 MiB of HBM per device.

```python
import math
import jax
import jax.numpy as jnp
import numpy as np
from jax import lax

D = 7168
H = 2048
EXP_NODE = 2
NODES_TOK = 4
SINK = 3
MB = 2
TOK_DEV = 4
HS = 1024
EXPERTS = 16
TOKENS = 64
CAP = 3
N_NODE = 8


def steps_of(own_key, dims, split, low, top_value):
    gain, own = 1.0, jax.random.fold_in(own_key, 6)
    for position, blocks in split:
        heights = jnp.exp(jax.random.uniform(jax.random.fold_in(own, position), (blocks,), jnp.float32, low / len(split), top_value / len(split)))
        gain = gain * jnp.repeat(heights, dims[position] // blocks).reshape([-1 if axis == position else 1 for axis in range(len(dims))])
    return gain


def assign_block(key, own, number, rows, amount, top, limit, lean):
    ranking = jax.random.permutation(key, amount)
    crowded, common = portions_of(amount, rows * top, limit, lean, True), portions_of(amount, rows * top, limit, lean, False)
    places = jnp.arange(amount)

    def named(sizes, offset_by):
        used = int((sizes > 0).sum())
        fixed = max(1, used // 4)
        shifted = fixed + (places - fixed + offset_by * (used - fixed)) % max(1, amount - fixed)
        return jnp.zeros((amount,), jnp.int32).at[ranking[jnp.where(places < fixed, places, shifted)]].set(jnp.asarray(sizes, jnp.int32))

    sizes = jnp.where(number % 4 == 0, named(crowded, number // 4), named(common, number - number // 4 - 1))
    mixed = jax.random.permutation(jax.random.fold_in(own, 3), amount)
    source_of, taker = mixed[0:amount // 2 * 2:2], mixed[1:amount // 2 * 2:2]
    margin = jnp.minimum(sizes[source_of] - 1, limit - sizes[taker]) // 2
    margin = jnp.where((source_of == ranking[0]) | (taker == ranking[0]) | (sizes[taker] == 0), 0, jnp.maximum(margin, 0))
    shifted = jax.random.randint(jax.random.fold_in(own, 4), (amount // 2,), 0, 1 << 20) % (margin + 1)
    sizes = sizes.at[source_of].add(-shifted).at[taker].add(shifted)
    items = jnp.searchsorted(jnp.cumsum(sizes), jnp.arange(rows * top), side="right").astype(jnp.int32)
    table = items.reshape(top, rows).T
    table = table[jax.random.permutation(jax.random.fold_in(own, 1), rows)]
    offset_by = jax.random.randint(jax.random.fold_in(own, 2), (rows, 1), 0, top)
    return jnp.take_along_axis(table, (jnp.arange(top)[None, :] + offset_by) % top, axis=1)


def portions_of(amount, total, bound, skew, full):
    loads = [(1 << 20) // math.isqrt(standing ** skew) + 1 for standing in range(1, amount + 1)]
    largest = bound if full else min(bound, max(-(-total // amount), total * loads[0] // sum(loads)))
    least = 1 if total - largest >= amount - 1 else 0
    holding, spare = [largest] + [least] * (amount - 1), total - largest - least * (amount - 1)
    while spare > 0:
        candidates = [i for i in range(1, amount) if holding[i] < largest] or [i for i in range(1, amount) if holding[i] < bound]
        whole, budget = sum([loads[i] for i in candidates]), spare
        for i in candidates:
            extra = min(bound - holding[i], max(1, budget * loads[i] // whole), spare)
            holding[i] = holding[i] + extra
            spare = spare - extra
    return np.array(holding)


def scatter_about(stream_key, shape, deviation, limit, shards=(), kind=jnp.bfloat16):
    values = jax.random.normal(stream_key, shape, jnp.float32) * deviation
    if len(shards) > 0:
        values = steps_of(stream_key, shape, shards, -0.22, 0.18) * values
    return jnp.clip(values, min=-limit, max=limit).astype(kind)


def setup_inputs(seed: int = 0, part: int = 0) -> dict:
    arg_keys = jax.random.split(jax.random.key(seed), 7)
    part_keys = jax.random.split(jax.random.fold_in(arg_keys[6], part), 7)
    tokens = scatter_about(part_keys[0], (MB, TOKENS, D), 1.0, 6.0, ((1, 16),))
    router = scatter_about(arg_keys[1], (D, EXPERTS), (D // 16) ** -0.5, 0.25)
    w_gate = scatter_about(arg_keys[2], (EXPERTS, D, H), D ** -0.5, 0.0625, ((0, 8), (2, 2)))
    w_up = scatter_about(arg_keys[3], (EXPERTS, D, H), D ** -0.5, 0.0625, ((0, 8), (2, 2)))
    w_down = scatter_about(arg_keys[4], (EXPERTS, H, D), (H // 4) ** -0.5, 0.25, ((0, 8), (1, 2)))
    node_lists_keys = jax.random.split(jax.random.fold_in(part_keys[5], 1), MB * TOKENS // TOK_DEV)
    node_lists_turns = jax.random.permutation(jax.random.fold_in(part_keys[5], 3), MB * TOKENS // TOK_DEV)
    node_lists = jax.vmap(lambda own, number: assign_block(jax.random.fold_in(part_keys[5], 2), own, number, TOK_DEV, N_NODE, NODES_TOK, CAP, 2))(node_lists_keys, node_lists_turns).reshape((MB, TOKENS, NODES_TOK))
    return dict(tokens=tokens, router=router, w_gate=w_gate, w_up=w_up, w_down=w_down, node_lists=node_lists)


def reference(tokens, router, w_gate, w_up, w_down, node_lists):
    node_ids = jnp.arange(N_NODE, dtype=jnp.int32)
    results = []
    for micro_batch in range(MB):
        token_rows = tokens[micro_batch]
        logits = jnp.dot(token_rows, router, preferred_element_type=jnp.float32)
        scores = jax.nn.sigmoid(logits)
        for sweep in range(SINK):
            scores = scores / jnp.sum(scores, axis=1, keepdims=True)
            scores = scores / jnp.sum(scores, axis=0, keepdims=True)
        chosen = jnp.sum((node_lists[micro_batch][:, :, None] == node_ids[None, None, :]).astype(jnp.float32), axis=1)
        picked = jnp.repeat(chosen, EXP_NODE, axis=1) * scores
        gate_vals = (picked / jnp.sum(picked, axis=1, keepdims=True)).astype(jnp.bfloat16)
        wide_rows = token_rows.astype(jnp.float32)

        def add_group(group, running):
            first = (group * EXP_NODE).astype(jnp.int32)
            gate_mat = lax.dynamic_slice_in_dim(w_gate, first, EXP_NODE, 0).astype(jnp.float32)
            up_mat = lax.dynamic_slice_in_dim(w_up, first, EXP_NODE, 0).astype(jnp.float32)
            down_mat = lax.dynamic_slice_in_dim(w_down, first, EXP_NODE, 0).astype(jnp.float32)
            weight_cols = lax.dynamic_slice_in_dim(gate_vals, first, EXP_NODE, 1).astype(jnp.float32)
            pre_gate = jnp.einsum("td,edh->eth", wide_rows, gate_mat)
            pre_up = jnp.einsum("td,edh->eth", wide_rows, up_mat)
            hidden = (jnp.transpose(weight_cols)[:, :, None] * jax.nn.silu(pre_gate) * pre_up).astype(jnp.bfloat16)
            hidden = hidden.astype(jnp.float32).reshape(EXP_NODE, TOKENS, H // HS, HS)
            down_blocks = down_mat.reshape(EXP_NODE, H // HS, HS, D)
            parts = jnp.einsum("etjh,ejhd->jtd", hidden, down_blocks)
            rounded = lax.optimization_barrier(parts.astype(jnp.bfloat16)).astype(jnp.float32)
            return running + jnp.sum(rounded, axis=0)

        mixed = lax.fori_loop(0, N_NODE, add_group, jnp.zeros((TOKENS, D), jnp.float32))
        results.append(mixed.astype(jnp.bfloat16))
    return jnp.stack(results)
```

```python
import jax
import jax.numpy as jnp
from jax import lax
from jax.experimental import pallas as pl
from jax.experimental.pallas import tpu as pltpu
from jax.sharding import PartitionSpec as P

NODES_TOK = 4
SINK = 3


def expert_term(rows_in, gate_in, w_gate, w_up, w_down):
    pre_gate = jnp.einsum("rd,edh->erh", rows_in, w_gate, preferred_element_type=jnp.float32)
    pre_up = jnp.einsum("rd,edh->erh", rows_in, w_up, preferred_element_type=jnp.float32)
    weight_rows = jnp.transpose(gate_in).astype(jnp.float32)[:, :, None]
    hidden = (weight_rows * jax.nn.silu(pre_gate) * pre_up).astype(jnp.bfloat16)
    return jnp.einsum("erh,ehd->rd", hidden, w_down, preferred_element_type=jnp.float32)


def build_slots(chosen_int, capacity):
    before = jnp.cumsum(chosen_int, axis=1) - chosen_int
    slot_ids = jnp.arange(capacity, dtype=jnp.int32)
    marks = (before[..., None] == slot_ids).astype(jnp.int32) * chosen_int[..., None]
    return marks.astype(jnp.bfloat16)


def node_first(rows_in, gate_vals, slot_marks, w_gate, w_up, w_down):
    micro_count, tok_count, node_count, capacity = slot_marks.shape
    experts_here = w_gate.shape[0]
    gate_split = gate_vals.reshape(micro_count, tok_count, node_count, experts_here)
    send_rows = jnp.einsum(
        "btmc,btd->bmcd", slot_marks, rows_in, preferred_element_type=jnp.float32
    ).astype(jnp.bfloat16)
    send_gates = jnp.einsum(
        "btmc,btmi->bmci", slot_marks, gate_split, preferred_element_type=jnp.float32
    ).astype(jnp.bfloat16)
    recv_rows, recv_gates = (
        lax.all_to_all(send_rows, "node", split_axis=1, concat_axis=1, tiled=True),
        lax.all_to_all(send_gates, "node", split_axis=1, concat_axis=1, tiled=True),
    )
    flat_rows = micro_count * node_count * capacity
    all_rows, all_gates = (
        lax.all_gather(recv_rows.reshape(flat_rows, -1), "local", axis=0, tiled=True),
        lax.all_gather(recv_gates.reshape(flat_rows, experts_here), "local", axis=0, tiled=True),
    )
    summed = lax.psum_scatter(
        expert_term(all_rows, all_gates, w_gate, w_up, w_down).astype(jnp.bfloat16),
        "local",
        scatter_dimension=0,
        tiled=True,
    ).astype(jnp.float32)
    returned = lax.all_to_all(
        summed.reshape(micro_count, node_count, capacity, -1).astype(jnp.bfloat16),
        "node",
        split_axis=1,
        concat_axis=1,
        tiled=True,
    ).astype(jnp.float32)
    return jnp.einsum(
        "btmc,bmcd->btd", slot_marks.astype(jnp.float32), returned, precision=lax.Precision.HIGHEST
    )


def route_rows(rows_in, gate_vals, slot_marks, w_gate, w_up, w_down):
    result = node_first(rows_in, gate_vals, slot_marks, w_gate, w_up, w_down)
    return result


def local(tokens, router, w_gate, w_up, w_down, node_lists):
    micro_count, tok_count, model_width = tokens.shape
    node_count = lax.axis_size("node")
    expert_count = router.shape[1]
    capacity = min(tok_count, tok_count * NODES_TOK // node_count + max(1, tok_count // 4))
    logits = jnp.einsum("btd,de->bte", tokens, router, preferred_element_type=jnp.float32)
    scores = jax.nn.sigmoid(logits)
    for sweep in range(SINK):
        scores = scores / jnp.sum(scores, axis=2, keepdims=True)
        scores = scores / lax.psum(jnp.sum(scores, axis=1), ("node", "local"))[:, None, :]
    node_ids = jnp.arange(node_count, dtype=jnp.int32)
    chosen_int = jnp.sum((node_lists[..., None] == node_ids).astype(jnp.int32), axis=2)
    picked = jnp.repeat(chosen_int.astype(jnp.float32), expert_count // node_count, axis=2) * scores
    gate_vals = (picked / jnp.sum(picked, axis=2, keepdims=True)).astype(jnp.bfloat16)
    slot_marks = build_slots(chosen_int, capacity)
    outputs = []
    for micro in range(micro_count):
        outputs.append(
            route_rows(
                tokens[micro : micro + 1],
                gate_vals[micro : micro + 1],
                slot_marks[micro : micro + 1],
                w_gate,
                w_up,
                w_down,
            )
        )
    mixed = jnp.concatenate(outputs, axis=0)
    return mixed.astype(jnp.bfloat16)


MESH = pl.DeviceIdType.MESH
BLK = 1024
PAIRS = 12


def fused_kernel(
    tok_ref, list_ref, router_hbm, gate_hbm, up_hbm, down_hbm, out_ref,
    wbuf, router_buf, xg, mg, xs, acc, hid, part, sib_in, mid, x_in, fin, z_in,
    w_sem, router_sem, gz_send, gz_recv, gx_send, gx_recv, gs_send, gs_recv,
    rs_send, rs_recv, rx_send, rx_recv, rz_send, rz_recv,
):
    width = tok_ref.shape[2]
    chunks = width // BLK
    experts_here = gate_hbm.shape[0]
    zs = xg.shape[3]
    half = BLK // 2
    grp, node, core = lax.axis_index("groups"), lax.axis_index("node"), lax.axis_index("local")
    zi, xi = node // 2, node % 2
    sib = (grp, node, 1 - core)
    xnb = (grp, zi * 2 + (1 - xi), core)

    def z_at(step):
        return (zi + step) % zs

    def znb(step):
        return (grp, z_at(step) * 2 + xi, core)

    def first_copy(pair, slot, kind):
        k, e = pair // 2, pair % 2
        rows = pl.ds(pl.multiple_of(k * BLK, BLK), BLK)
        source = (gate_hbm, up_hbm)[kind].at[e, rows, :]
        return pltpu.make_async_copy(source, wbuf.at[slot, kind], w_sem.at[slot, kind])

    def down_copies(q, slot):
        cols = pl.ds(pl.multiple_of(q * BLK, BLK), BLK)
        return (
            pltpu.make_async_copy(down_hbm.at[0, :, cols], wbuf.at[slot, 0], w_sem.at[slot, 0]),
            pltpu.make_async_copy(down_hbm.at[1, :, cols], wbuf.at[slot, 1], w_sem.at[slot, 1]),
        )

    router_copy = pltpu.make_async_copy(router_hbm, router_buf, router_sem)
    router_copy.start()

    @pl.loop(0, PAIRS)
    def _(pair):
        for kind in range(2):
            first_copy(pair, pair, kind).start()

    rows_own = jnp.concatenate(
        [tok_ref[0].astype(jnp.float32), tok_ref[1].astype(jnp.float32)], axis=0
    )
    for k in range(chunks):
        left = rows_own[:, k * BLK : k * BLK + half]
        right = rows_own[:, k * BLK + half : (k + 1) * BLK]
        xg[k, core, xi, zi] = jnp.concatenate([left, right], axis=0).astype(jnp.bfloat16)

    barrier = pltpu.get_barrier_semaphore()
    peers = [sib, xnb] + [znb(step) for step in range(1, zs)]
    for peer in peers:
        pl.semaphore_signal(barrier, inc=1, device_id=peer, device_id_type=MESH)
    pl.semaphore_wait(barrier, len(peers))

    def remote(src, dst, send, recv, peer):
        return pltpu.make_async_remote_copy(
            src_ref=src, dst_ref=dst, send_sem=send, recv_sem=recv, device_id=peer, device_id_type=MESH
        )

    def slot_of(k):
        return mg if k is None else xg.at[k]

    def sem_of(k):
        return chunks if k is None else k

    def gather_z(k, step):
        place = slot_of(k).at[core, xi, zi]
        return remote(place, place, gz_send.at[sem_of(k), step - 1], gz_recv.at[sem_of(k), step - 1], znb(step))

    def gather_x(k):
        place = slot_of(k).at[core, xi]
        return remote(place, place, gx_send.at[sem_of(k)], gx_recv.at[sem_of(k)], xnb)

    def gather_s(k):
        place = slot_of(k).at[core]
        return remote(place, place, gs_send.at[sem_of(k)], gs_recv.at[sem_of(k)], sib)

    def start_z(k):
        for step in range(1, zs):
            gather_z(k, step).start()

    def relay_x(k):
        for step in range(1, zs):
            gather_z(k, step).wait_recv()
        gather_x(k).start()

    def relay_s(k):
        gather_x(k).wait_recv()
        gather_s(k).start()

    @pl.loop(0, chunks)
    def _(k):
        start_z(k)

    router_copy.wait()
    logits = jnp.dot(rows_own.astype(jnp.bfloat16), router_buf[...], preferred_element_type=jnp.float32)
    experts = logits.shape[1]
    logits = jnp.concatenate([logits, jnp.zeros((logits.shape[0], 128 - experts), jnp.float32)], axis=1)
    marks = []
    group_of = lax.broadcasted_iota(jnp.int32, (tok_ref.shape[1], 128), 1) // experts_here
    for b in range(2):
        names = list_ref[b]
        total = jnp.zeros(group_of.shape, jnp.float32)
        for j in range(names.shape[1]):
            total = total + (names[:, j : j + 1] == group_of).astype(jnp.float32)
        marks.append(total)
    mg[core, xi, zi] = jnp.concatenate([logits] + marks, axis=0)
    start_z(None)

    relay_x(0)

    @pl.loop(1, chunks)
    def _(k):
        relay_x(k)
        relay_s(k - 1)

    relay_x(None)
    relay_s(chunks - 1)
    relay_s(None)

    rows = 2 * 2 * zs * 8
    acc[...] = jnp.zeros_like(acc)

    @pl.loop(0, chunks * 2)
    def _(pair):
        k, e = pair // 2, pair % 2
        slot = pair % PAIRS

        @pl.when(e == 0)
        def _():
            gather_s(k).wait_recv()
            wide = xg[k].astype(jnp.float32).reshape(2 * 2 * zs, 16, half)
            xs[:, :half] = wide[:, :8].reshape(rows, half).astype(jnp.bfloat16)
            xs[:, half:] = wide[:, 8:].reshape(rows, half).astype(jnp.bfloat16)

        for kind in range(2):
            first_copy(pair, slot, kind).wait()

            @pl.loop(0, BLK // 256)
            def _(n):
                cols = pl.ds(pl.multiple_of(n * 256, 256), 256)
                acc[e, kind, :, cols] += jnp.dot(
                    xs[...], wbuf[slot, kind, :, cols], preferred_element_type=jnp.float32
                )

        later = pair + PAIRS

        @pl.when(later < chunks * 2)
        def _():
            for kind in range(2):
                first_copy(later, slot, kind).start()

        @pl.when((later >= chunks * 2) & (later < chunks * 3))
        def _():
            for copy in down_copies(later - chunks * 2, slot):
                copy.start()

    gather_s(None).wait_recv()
    meta = mg[...].reshape(2 * 2 * zs, 16, 128)
    lane = lax.broadcasted_iota(jnp.int32, (rows, 128), 1)
    real = lane < experts
    first = (lax.broadcasted_iota(jnp.int32, (rows, 128), 0) // 4) % 2 == 0
    scores = 1.0 / (1.0 + jnp.exp(-meta[:, :8].reshape(rows, 128)))
    scores = jnp.where(real, scores, 0.0)
    for sweep in range(SINK):
        scores = scores / jnp.sum(scores, axis=1, keepdims=True)
        sum_a = jnp.sum(jnp.where(first, scores, 0.0), axis=0, keepdims=True)
        sum_b = jnp.sum(jnp.where(first, 0.0, scores), axis=0, keepdims=True)
        scores = scores / jnp.where(real, jnp.where(first, sum_a, sum_b), 1.0)
    picked = meta[:, 8:].reshape(rows, 128) * scores
    gates = (picked / jnp.sum(picked, axis=1, keepdims=True)).astype(jnp.bfloat16).astype(jnp.float32)
    for e in range(experts_here):
        weight = jnp.sum(jnp.where(lane == node * experts_here + e, gates, 0.0), axis=1, keepdims=True)

        @pl.loop(0, BLK // 256)
        def _(n):
            cols = pl.ds(pl.multiple_of(n * 256, 256), 256)
            pre = acc[e, 0, :, cols]
            hid[e, :, cols] = (weight * (pre / (1.0 + jnp.exp(-pre))) * acc[e, 1, :, cols]).astype(jnp.bfloat16)

    def reduce_s(q):
        return remote(part.at[q, 1 - core], sib_in.at[q], rs_send.at[q], rs_recv.at[q], sib)

    def reduce_x(q):
        return remote(mid.at[q, 1 - xi], x_in.at[q], rx_send.at[q], rx_recv.at[q], xnb)

    def reduce_z(q, step):
        return remote(
            fin.at[q, z_at(step)], z_in.at[q, step - 1], rz_send.at[q, step - 1], rz_recv.at[q, step - 1], znb(step)
        )

    def multiply(q):
        slot = (chunks * 2 + q) % PAIRS
        for copy in down_copies(q, slot):
            copy.wait()
        for side in range(2):
            for n in range(half // 256):
                cols = slice(side * half + n * 256, side * half + (n + 1) * 256)
                value = jnp.dot(hid[0], wbuf[slot, 0, :, cols], preferred_element_type=jnp.float32)
                value = value + jnp.dot(hid[1], wbuf[slot, 1, :, cols], preferred_element_type=jnp.float32)
                acc[0, side, :, n * 256 : (n + 1) * 256] = value
        low = acc[0, 0, :, :half].reshape(2 * 2 * zs, 8, half)
        high = acc[0, 1, :, :half].reshape(2 * 2 * zs, 8, half)
        part[q] = jnp.concatenate([low, high], axis=1).reshape(2, 2, zs, 16, half).astype(jnp.bfloat16)
        reduce_s(q).start()

    def add_pair(q):
        reduce_s(q).wait_recv()
        mid[q] = (part[q, core].astype(jnp.float32) + sib_in[q].astype(jnp.float32)).astype(jnp.bfloat16)
        reduce_x(q).start()

    def add_x(q):
        reduce_x(q).wait_recv()
        fin[q] = (mid[q, xi].astype(jnp.float32) + x_in[q].astype(jnp.float32)).astype(jnp.bfloat16)
        for step in range(1, zs):
            reduce_z(q, step).start()

    def add_z(q):
        total = fin[q, zi].astype(jnp.float32)
        for step in range(1, zs):
            reduce_z(q, step).wait_recv()
            total = total + z_in[q, step - 1].astype(jnp.float32)
        for side in range(2):
            cols = pl.ds(pl.multiple_of(q * BLK + side * half, half), half)
            for b in range(2):
                row = side * 8 + b * 4
                out_ref[b, :, cols] = total[row : row + 4].astype(jnp.bfloat16)

    @pl.loop(0, chunks + 3)
    def _(q):
        @pl.when(q < chunks)
        def _():
            multiply(q)

        @pl.when((q >= 1) & (q < chunks + 1))
        def _():
            add_pair(q - 1)

        @pl.when((q >= 2) & (q < chunks + 2))
        def _():
            add_x(q - 2)

        @pl.when(q >= 3)
        def _():
            add_z(q - 3)

    @pl.loop(0, chunks)
    def _(k):
        for step in range(1, zs):
            gather_z(k, step).wait_send()
            reduce_z(k, step).wait_send()
        gather_x(k).wait_send()
        gather_s(k).wait_send()
        reduce_s(k).wait_send()
        reduce_x(k).wait_send()

    for step in range(1, zs):
        gather_z(None, step).wait_send()
    gather_x(None).wait_send()
    gather_s(None).wait_send()


def fused(tokens, router, w_gate, w_up, w_down, node_lists):
    width = tokens.shape[2]
    chunks = width // BLK
    zs = lax.axis_size("node") // 2
    half = BLK // 2
    rows = 2 * 2 * zs * 8
    bf16, f32 = jnp.bfloat16, jnp.float32
    dma = pltpu.SemaphoreType.DMA
    any_spec = pl.BlockSpec(memory_space=pl.ANY)
    vmem_spec = pl.BlockSpec(memory_space=pltpu.VMEM)
    return pl.pallas_call(
        fused_kernel,
        out_shape=jax.ShapeDtypeStruct(tokens.shape, tokens.dtype),
        in_specs=[vmem_spec, vmem_spec, any_spec, any_spec, any_spec, any_spec],
        out_specs=vmem_spec,
        scratch_shapes=[
            pltpu.VMEM((PAIRS, 2, BLK, BLK), bf16),
            pltpu.VMEM(router.shape, bf16),
            pltpu.VMEM((chunks, 2, 2, zs, 16, half), bf16),
            pltpu.VMEM((2, 2, zs, 16, 128), f32),
            pltpu.VMEM((rows, BLK), bf16),
            pltpu.VMEM((2, 2, rows, BLK), f32),
            pltpu.VMEM((2, rows, BLK), bf16),
            pltpu.VMEM((chunks, 2, 2, zs, 16, half), bf16),
            pltpu.VMEM((chunks, 2, zs, 16, half), bf16),
            pltpu.VMEM((chunks, 2, zs, 16, half), bf16),
            pltpu.VMEM((chunks, zs, 16, half), bf16),
            pltpu.VMEM((chunks, zs, 16, half), bf16),
            pltpu.VMEM((chunks, zs - 1, 16, half), bf16),
            dma((PAIRS, 2)),
            dma,
            dma((chunks + 1, zs - 1)), dma((chunks + 1, zs - 1)),
            dma((chunks + 1,)), dma((chunks + 1,)),
            dma((chunks + 1,)), dma((chunks + 1,)),
            dma((chunks,)), dma((chunks,)),
            dma((chunks,)), dma((chunks,)),
            dma((chunks, zs - 1)), dma((chunks, zs - 1)),
        ],
        compiler_params=pltpu.CompilerParams(
            collective_id=0, has_side_effects=True, vmem_limit_bytes=63 * 1024 * 1024
        ),
        cost_estimate=pl.CostEstimate(
            flops=12 * rows * width * BLK, bytes_accessed=12 * width * BLK, transcendentals=2 * rows * BLK
        ),
    )(tokens, node_lists, router, w_gate, w_up, w_down)


def solution(mesh):
    def body(tokens, router, w_gate, w_up, w_down, node_lists):
        fits = (
            mesh.shape["local"] == 2
            and mesh.shape["node"] % 2 == 0
            and tokens.shape[:2] == (2, 4)
            and w_gate.shape[0] == 2
            and w_gate.shape[2] == BLK
            and tokens.shape[2] % BLK == 0
        )
        plan = fused if fits else local
        return plan(tokens, router, w_gate, w_up, w_down, node_lists)

    return jax.shard_map(
        body,
        mesh=mesh,
        in_specs=(
            P(None, ("groups", "node", "local"), None),
            P(),
            P("node", None, "local"),
            P("node", None, "local"),
            P("node", "local", None),
            P(None, ("groups", "node", "local"), None),
        ),
        out_specs=P(None, ("groups", "node", "local"), None),
        check_vma=False,
    )
```

```python
import jax
import jax.numpy as jnp
from jax import lax
from jax.experimental import pallas as pl
from jax.experimental.pallas import tpu as pltpu
from jax.sharding import PartitionSpec as P

NODES_TOK = 4
SINK = 3


def expert_term(rows_in, gate_in, w_gate, w_up, w_down):
    pre_gate = jnp.einsum("rd,edh->erh", rows_in, w_gate, preferred_element_type=jnp.float32)
    pre_up = jnp.einsum("rd,edh->erh", rows_in, w_up, preferred_element_type=jnp.float32)
    weight_rows = jnp.transpose(gate_in).astype(jnp.float32)[:, :, None]
    hidden = (weight_rows * jax.nn.silu(pre_gate) * pre_up).astype(jnp.bfloat16)
    return jnp.einsum("erh,ehd->rd", hidden, w_down, preferred_element_type=jnp.float32)


def build_slots(chosen_int, capacity):
    before = jnp.cumsum(chosen_int, axis=1) - chosen_int
    slot_ids = jnp.arange(capacity, dtype=jnp.int32)
    marks = (before[..., None] == slot_ids).astype(jnp.int32) * chosen_int[..., None]
    return marks.astype(jnp.bfloat16)


def node_first(rows_in, gate_vals, slot_marks, w_gate, w_up, w_down):
    micro_count, tok_count, node_count, capacity = slot_marks.shape
    experts_here = w_gate.shape[0]
    gate_split = gate_vals.reshape(micro_count, tok_count, node_count, experts_here)
    send_rows = jnp.einsum(
        "btmc,btd->bmcd", slot_marks, rows_in, preferred_element_type=jnp.float32
    ).astype(jnp.bfloat16)
    send_gates = jnp.einsum(
        "btmc,btmi->bmci", slot_marks, gate_split, preferred_element_type=jnp.float32
    ).astype(jnp.bfloat16)
    recv_rows, recv_gates = (
        lax.all_to_all(send_rows, "node", split_axis=1, concat_axis=1, tiled=True),
        lax.all_to_all(send_gates, "node", split_axis=1, concat_axis=1, tiled=True),
    )
    flat_rows = micro_count * node_count * capacity
    all_rows, all_gates = (
        lax.all_gather(recv_rows.reshape(flat_rows, -1), "local", axis=0, tiled=True),
        lax.all_gather(recv_gates.reshape(flat_rows, experts_here), "local", axis=0, tiled=True),
    )
    summed = lax.psum_scatter(
        expert_term(all_rows, all_gates, w_gate, w_up, w_down).astype(jnp.bfloat16),
        "local",
        scatter_dimension=0,
        tiled=True,
    ).astype(jnp.float32)
    returned = lax.all_to_all(
        summed.reshape(micro_count, node_count, capacity, -1).astype(jnp.bfloat16),
        "node",
        split_axis=1,
        concat_axis=1,
        tiled=True,
    ).astype(jnp.float32)
    return jnp.einsum(
        "btmc,bmcd->btd", slot_marks.astype(jnp.float32), returned, precision=lax.Precision.HIGHEST
    )


def route_rows(rows_in, gate_vals, slot_marks, w_gate, w_up, w_down):
    result = node_first(rows_in, gate_vals, slot_marks, w_gate, w_up, w_down)
    return result


def local(tokens, router, w_gate, w_up, w_down, node_lists):
    micro_count, tok_count, model_width = tokens.shape
    node_count = lax.axis_size("node")
    expert_count = router.shape[1]
    capacity = min(tok_count, tok_count * NODES_TOK // node_count + max(1, tok_count // 4))
    logits = jnp.einsum("btd,de->bte", tokens, router, preferred_element_type=jnp.float32)
    scores = jax.nn.sigmoid(logits)
    for sweep in range(SINK):
        scores = scores / jnp.sum(scores, axis=2, keepdims=True)
        scores = scores / lax.psum(jnp.sum(scores, axis=1), ("node", "local"))[:, None, :]
    node_ids = jnp.arange(node_count, dtype=jnp.int32)
    chosen_int = jnp.sum((node_lists[..., None] == node_ids).astype(jnp.int32), axis=2)
    picked = jnp.repeat(chosen_int.astype(jnp.float32), expert_count // node_count, axis=2) * scores
    gate_vals = (picked / jnp.sum(picked, axis=2, keepdims=True)).astype(jnp.bfloat16)
    slot_marks = build_slots(chosen_int, capacity)
    outputs = []
    for micro in range(micro_count):
        outputs.append(
            route_rows(
                tokens[micro : micro + 1],
                gate_vals[micro : micro + 1],
                slot_marks[micro : micro + 1],
                w_gate,
                w_up,
                w_down,
            )
        )
    mixed = jnp.concatenate(outputs, axis=0)
    return mixed.astype(jnp.bfloat16)


MESH = pl.DeviceIdType.MESH
BLK = 1024
PAIRS = 12


def fused_kernel(
    tok_ref, list_ref, router_hbm, gate_hbm, up_hbm, down_hbm, out_ref,
    wbuf, router_buf, xg, mg, xs, acc, hid, part, sib_in, mid, x_in, fin, z_in,
    w_sem, router_sem, gz_send, gz_recv, gx_send, gx_recv, gs_send, gs_recv,
    rs_send, rs_recv, rx_send, rx_recv, rz_send, rz_recv,
):
    width = tok_ref.shape[2]
    chunks = width // BLK
    experts_here = gate_hbm.shape[0]
    zs = xg.shape[3]
    half = BLK // 2
    grp, node, core = lax.axis_index("groups"), lax.axis_index("node"), lax.axis_index("local")
    zi, xi = node // 2, node % 2
    sib = (grp, node, 1 - core)
    xnb = (grp, zi * 2 + (1 - xi), core)

    def z_at(step):
        return (zi + step) % zs

    def znb(step):
        return (grp, z_at(step) * 2 + xi, core)

    def first_copy(pair, slot, kind):
        k, e = pair // 2, pair % 2
        rows = pl.ds(pl.multiple_of(k * BLK, BLK), BLK)
        source = (gate_hbm, up_hbm)[kind].at[e, rows, :]
        return pltpu.make_async_copy(source, wbuf.at[slot, kind], w_sem.at[slot, kind])

    def down_copies(q, slot):
        cols = pl.ds(pl.multiple_of(q * BLK, BLK), BLK)
        return (
            pltpu.make_async_copy(down_hbm.at[0, :, cols], wbuf.at[slot, 0], w_sem.at[slot, 0]),
            pltpu.make_async_copy(down_hbm.at[1, :, cols], wbuf.at[slot, 1], w_sem.at[slot, 1]),
        )

    router_copy = pltpu.make_async_copy(router_hbm, router_buf, router_sem)
    router_copy.start()

    @pl.loop(0, PAIRS)
    def _(pair):
        for kind in range(2):
            first_copy(pair, pair, kind).start()

    rows_own = jnp.concatenate(
        [tok_ref[0].astype(jnp.float32), tok_ref[1].astype(jnp.float32)], axis=0
    )
    for k in range(chunks):
        left = rows_own[:, k * BLK : k * BLK + half]
        right = rows_own[:, k * BLK + half : (k + 1) * BLK]
        xg[k, core, xi, zi] = jnp.concatenate([left, right], axis=0).astype(jnp.bfloat16)

    barrier = pltpu.get_barrier_semaphore()
    peers = [sib, xnb] + [znb(step) for step in range(1, zs)]
    for peer in peers:
        pl.semaphore_signal(barrier, inc=1, device_id=peer, device_id_type=MESH)
    pl.semaphore_wait(barrier, len(peers))

    def remote(src, dst, send, recv, peer):
        return pltpu.make_async_remote_copy(
            src_ref=src, dst_ref=dst, send_sem=send, recv_sem=recv, device_id=peer, device_id_type=MESH
        )

    def slot_of(k):
        return mg if k is None else xg.at[k]

    def sem_of(k):
        return chunks if k is None else k

    def gather_z(k, step):
        place = slot_of(k).at[core, xi, zi]
        return remote(place, place, gz_send.at[sem_of(k), step - 1], gz_recv.at[sem_of(k), step - 1], znb(step))

    def gather_x(k):
        place = slot_of(k).at[core, xi]
        return remote(place, place, gx_send.at[sem_of(k)], gx_recv.at[sem_of(k)], xnb)

    def gather_s(k):
        place = slot_of(k).at[core]
        return remote(place, place, gs_send.at[sem_of(k)], gs_recv.at[sem_of(k)], sib)

    def start_z(k):
        for step in range(1, zs):
            gather_z(k, step).start()

    def relay_x(k):
        for step in range(1, zs):
            gather_z(k, step).wait_recv()
        gather_x(k).start()

    def relay_s(k):
        gather_x(k).wait_recv()
        gather_s(k).start()

    start_z(0)
    start_z(1)

    router_copy.wait()
    logits = lax.dot_general(
        rows_own.astype(jnp.bfloat16), router_buf[...], (((1,), (1,)), ((), ())), preferred_element_type=jnp.float32
    )
    experts = logits.shape[1]
    logits = jnp.concatenate([logits, jnp.zeros((logits.shape[0], 128 - experts), jnp.float32)], axis=1)
    marks = []
    group_of = lax.broadcasted_iota(jnp.int32, (tok_ref.shape[1], 128), 1) // experts_here
    for b in range(2):
        names = list_ref[b]
        total = jnp.zeros(group_of.shape, jnp.float32)
        for j in range(names.shape[1]):
            total = total + (names[:, j : j + 1] == group_of).astype(jnp.float32)
        marks.append(total)
    mg[core, xi, zi] = jnp.concatenate([logits] + marks, axis=0)
    start_z(None)

    relay_x(0)
    start_z(2)
    relay_x(1)
    start_z(3)
    relay_s(0)
    relay_x(None)

    rows = 2 * 2 * zs * 8
    acc[...] = jnp.zeros_like(acc)

    @pl.loop(0, chunks * 2)
    def _(pair):
        k, e = pair // 2, pair % 2
        slot = pair % PAIRS

        @pl.when((e == 0) & (k + 2 < chunks))
        def _():
            relay_x(k + 2)

        @pl.when((e == 0) & (k + 4 < chunks))
        def _():
            start_z(k + 4)

        @pl.when((e == 0) & (k + 1 < chunks))
        def _():
            relay_s(k + 1)

        @pl.when(pair == 0)
        def _():
            relay_s(None)

        @pl.when(e == 0)
        def _():
            gather_s(k).wait_recv()
            wide = xg[k].astype(jnp.float32).reshape(2 * 2 * zs, 16, half)
            xs[:, :half] = wide[:, :8].reshape(rows, half).astype(jnp.bfloat16)
            xs[:, half:] = wide[:, 8:].reshape(rows, half).astype(jnp.bfloat16)

        for kind in range(2):
            first_copy(pair, slot, kind).wait()

            acc[e, kind] += jnp.dot(xs[...], wbuf[slot, kind], preferred_element_type=jnp.float32)

        later = pair + PAIRS

        @pl.when(later < chunks * 2)
        def _():
            for kind in range(2):
                first_copy(later, slot, kind).start()

        @pl.when((later >= chunks * 2) & (later < chunks * 3))
        def _():
            for copy in down_copies(later - chunks * 2, slot):
                copy.start()

    gather_s(None).wait_recv()
    meta = mg[...].reshape(2 * 2 * zs, 16, 128)
    lane = lax.broadcasted_iota(jnp.int32, (rows, 128), 1)
    real = lane < experts
    first = (lax.broadcasted_iota(jnp.int32, (rows, 128), 0) // 4) % 2 == 0
    scores = 1.0 / (1.0 + jnp.exp(-meta[:, :8].reshape(rows, 128)))
    scores = jnp.where(real, scores, 0.0)
    for sweep in range(SINK):
        scores = scores / jnp.sum(scores, axis=1, keepdims=True)
        sum_a = jnp.sum(jnp.where(first, scores, 0.0), axis=0, keepdims=True)
        sum_b = jnp.sum(jnp.where(first, 0.0, scores), axis=0, keepdims=True)
        scores = scores / jnp.where(real, jnp.where(first, sum_a, sum_b), 1.0)
    picked = meta[:, 8:].reshape(rows, 128) * scores
    gates = (picked / jnp.sum(picked, axis=1, keepdims=True)).astype(jnp.bfloat16).astype(jnp.float32)
    for e in range(experts_here):
        weight = jnp.sum(jnp.where(lane == node * experts_here + e, gates, 0.0), axis=1, keepdims=True)

        @pl.loop(0, BLK // 256)
        def _(n):
            cols = pl.ds(pl.multiple_of(n * 256, 256), 256)
            pre = acc[e, 0, :, cols]
            hid[e, :, cols] = (weight * (pre / (1.0 + jnp.exp(-pre))) * acc[e, 1, :, cols]).astype(jnp.bfloat16)

    def reduce_s(q):
        return remote(part.at[q, 1 - core], sib_in.at[q], rs_send.at[q], rs_recv.at[q], sib)

    def reduce_x(q):
        return remote(mid.at[q, 1 - xi], x_in.at[q], rx_send.at[q], rx_recv.at[q], xnb)

    def reduce_z(q, step):
        return remote(
            fin.at[q, z_at(step)], z_in.at[q, step - 1], rz_send.at[q, step - 1], rz_recv.at[q, step - 1], znb(step)
        )

    def multiply(q):
        slot = (chunks * 2 + q) % PAIRS
        for copy in down_copies(q, slot):
            copy.wait()
        value = jnp.dot(hid[0], wbuf[slot, 0], preferred_element_type=jnp.float32)
        value = value + jnp.dot(hid[1], wbuf[slot, 1], preferred_element_type=jnp.float32)
        low = value[:, :half].reshape(2 * 2 * zs, 8, half)
        high = value[:, half:].reshape(2 * 2 * zs, 8, half)
        part[q] = jnp.concatenate([low, high], axis=1).reshape(2, 2, zs, 16, half).astype(jnp.bfloat16)
        reduce_s(q).start()

    def add_pair(q):
        reduce_s(q).wait_recv()
        mid[q] = (part[q, core].astype(jnp.float32) + sib_in[q].astype(jnp.float32)).astype(jnp.bfloat16)
        reduce_x(q).start()

    def add_x(q):
        reduce_x(q).wait_recv()
        fin[q] = (mid[q, xi].astype(jnp.float32) + x_in[q].astype(jnp.float32)).astype(jnp.bfloat16)
        for step in range(1, zs):
            reduce_z(q, step).start()

    def add_z(q):
        total = fin[q, zi].astype(jnp.float32)
        for step in range(1, zs):
            reduce_z(q, step).wait_recv()
            total = total + z_in[q, step - 1].astype(jnp.float32)
        for side in range(2):
            cols = pl.ds(pl.multiple_of(q * BLK + side * half, half), half)
            for b in range(2):
                row = side * 8 + b * 4
                out_ref[b, :, cols] = total[row : row + 4].astype(jnp.bfloat16)

    @pl.loop(0, chunks + 5)
    def _(q):
        @pl.when(q < chunks)
        def _():
            multiply(q)

        @pl.when((q >= 1) & (q < chunks + 1))
        def _():
            add_pair(q - 1)

        @pl.when((q >= 3) & (q < chunks + 3))
        def _():
            add_x(q - 3)

        @pl.when(q >= 5)
        def _():
            add_z(q - 5)

    @pl.loop(0, chunks)
    def _(k):
        for step in range(1, zs):
            gather_z(k, step).wait_send()
            reduce_z(k, step).wait_send()
        gather_x(k).wait_send()
        gather_s(k).wait_send()
        reduce_s(k).wait_send()
        reduce_x(k).wait_send()

    for step in range(1, zs):
        gather_z(None, step).wait_send()
    gather_x(None).wait_send()
    gather_s(None).wait_send()


def fused(tokens, router, w_gate, w_up, w_down, node_lists):
    width = tokens.shape[2]
    chunks = width // BLK
    zs = lax.axis_size("node") // 2
    half = BLK // 2
    rows = 2 * 2 * zs * 8
    bf16, f32 = jnp.bfloat16, jnp.float32
    dma = pltpu.SemaphoreType.DMA
    any_spec = pl.BlockSpec(memory_space=pl.ANY)
    vmem_spec = pl.BlockSpec(memory_space=pltpu.VMEM)
    return pl.pallas_call(
        fused_kernel,
        out_shape=jax.ShapeDtypeStruct(tokens.shape, tokens.dtype),
        in_specs=[vmem_spec, vmem_spec, any_spec, any_spec, any_spec, any_spec],
        out_specs=vmem_spec,
        scratch_shapes=[
            pltpu.VMEM((PAIRS, 2, BLK, BLK), bf16),
            pltpu.VMEM(router.shape[::-1], bf16),
            pltpu.VMEM((chunks, 2, 2, zs, 16, half), bf16),
            pltpu.VMEM((2, 2, zs, 16, 128), f32),
            pltpu.VMEM((rows, BLK), bf16),
            pltpu.VMEM((2, 2, rows, BLK), f32),
            pltpu.VMEM((2, rows, BLK), bf16),
            pltpu.VMEM((chunks, 2, 2, zs, 16, half), bf16),
            pltpu.VMEM((chunks, 2, zs, 16, half), bf16),
            pltpu.VMEM((chunks, 2, zs, 16, half), bf16),
            pltpu.VMEM((chunks, zs, 16, half), bf16),
            pltpu.VMEM((chunks, zs, 16, half), bf16),
            pltpu.VMEM((chunks, zs - 1, 16, half), bf16),
            dma((PAIRS, 2)),
            dma,
            dma((chunks + 1, zs - 1)), dma((chunks + 1, zs - 1)),
            dma((chunks + 1,)), dma((chunks + 1,)),
            dma((chunks + 1,)), dma((chunks + 1,)),
            dma((chunks,)), dma((chunks,)),
            dma((chunks,)), dma((chunks,)),
            dma((chunks, zs - 1)), dma((chunks, zs - 1)),
        ],
        compiler_params=pltpu.CompilerParams(
            collective_id=0, has_side_effects=True, vmem_limit_bytes=63 * 1024 * 1024
        ),
        cost_estimate=pl.CostEstimate(
            flops=12 * rows * width * BLK, bytes_accessed=12 * width * BLK, transcendentals=2 * rows * BLK
        ),
    )(tokens, node_lists, jnp.transpose(router), w_gate, w_up, w_down)


def solution(mesh):
    def body(tokens, router, w_gate, w_up, w_down, node_lists):
        fits = (
            mesh.shape["local"] == 2
            and mesh.shape["node"] % 2 == 0
            and tokens.shape[:2] == (2, 4)
            and w_gate.shape[0] == 2
            and w_gate.shape[2] == BLK
            and tokens.shape[2] % BLK == 0
            and tokens.shape[2] // BLK >= 4
        )
        plan = fused if fits else local
        return plan(tokens, router, w_gate, w_up, w_down, node_lists)

    return jax.shard_map(
        body,
        mesh=mesh,
        in_specs=(
            P(None, ("groups", "node", "local"), None),
            P(),
            P("node", None, "local"),
            P("node", None, "local"),
            P("node", "local", None),
            P(None, ("groups", "node", "local"), None),
        ),
        out_specs=P(None, ("groups", "node", "local"), None),
        check_vma=False,
    )
```
